32 devices in a mesh: tile: 8 (over y, x, core), corner: 4 (over z).
Axes of the slice: x: 2, y: 2, z: 4, core: 2. Of those that a mesh axis runs over, the one named last changes fastest.
Arguments:
- mask: float32 [1024, 384], P('tile'), may hold values from 0 to 1
- target: int32 [1024, 384], P('tile'), may hold values 0 or 1
- pixel_weight: float32 [1024, 384], P('tile'), may hold values from 0.49 to 108
- row_taps: float32 [4, 8, 2, 129], replicated, may hold values from -2 to 2
- col_taps: float32 [4, 8, 2, 129], replicated, may hold values from -2 to 2
- kernel_weights: float32 [4, 8], replicated, may hold values from 0.03 to 0.25
- corner_set: int32 [16], P('corner'), may hold values from 0 to 3
- dose: float32 [16], P('corner'), may hold values from 0.8 to 1.25
Outputs:
- soft_error: float32 [1024, 384], P('tile')
- new_mask: float32 [1024, 384], P(('tile', 'corner'))
The draws below stay inside these ranges and needn't reach their ends.
Inputs may be any that keep to these rules, and one draw needn't show every extreme that they name: `corner_set`: each corner names one of 4 focus settings. target pixels are 0 or 1.
All inputs are finite; a program needn't handle non-finite values. No bound on the sum of `target` on one device may be relied on, other than what follows from the above.
Results may differ from the reference program's by a relative error of at most 0.0051.
Values may be sent and summed in bfloat16 or wider, within the bound.
A program may use at most 64 MiB of HBM per device.

```python
import math
import jax
import jax.numpy as jnp
from jax import lax

TH = 128
TW = 384
R = 64
K = 8
NSETS = 4
CORNERS = 16
ROWS = 1024


def draw_pixel_weight(key, part):
    key_pixel, key_column = jax.random.split(key)
    position = jnp.arange(ROWS, dtype=jnp.float32)[:, None] / float(max(ROWS - 1, 1))
    column = jnp.exp(jnp.log(3.0) * jax.random.uniform(key_column, (1, TW), jnp.float32))
    rising = 1.0 + 2.0 * position
    pixel = jnp.exp(0.35 * jnp.clip(jax.random.normal(key_pixel, (ROWS, TW), jnp.float32), -2.0, 2.0))
    return (rising * pixel * column).astype(jnp.float32)


def kernel_scale(key):
    weight_key = jax.random.fold_in(key, 7)
    uniform_draw = jax.random.uniform(weight_key, (NSETS, K), jnp.float32)
    return jnp.exp(jnp.log(0.03) + (jnp.log(0.25) - jnp.log(0.03)) * uniform_draw)


def draw_kernel_weights(key, part):
    return kernel_scale(key).astype(jnp.float32)


def kernel_taps(key, stream_salt):
    weights = kernel_scale(key)
    sharpness = jnp.clip(jnp.log(0.25 / weights) / jnp.log(0.25 / 0.03), 0.0, 1.0)[:, :, None, None]
    streams = jax.random.split(jax.random.fold_in(key, stream_salt), 9)
    tap_count = 2 * R + 1
    offset = jnp.arange(tap_count, dtype=jnp.float32) - float(R)
    position = offset / float(R)
    sign_flip = 1.0 - 2.0 * (jnp.arange(tap_count, dtype=jnp.int32) % 2).astype(jnp.float32)
    rotation = 2.0 * math.pi * jax.random.uniform(streams[0], (NSETS, K, 1, 1), jnp.float32)
    part_factor = jnp.concatenate([jnp.cos(rotation), jnp.sin(rotation)], axis=2)
    dc_level = 1.6 * (0.9 + 0.3 * jax.random.uniform(streams[1], (NSETS, K, 1, 1), jnp.float32)) * part_factor
    ripple_gain = 0.5 * jnp.clip(jax.random.normal(streams[2], (3, NSETS, K, 2, 1), jnp.float32), -2.5, 2.5)
    ripple_freq = 0.5 + 2.5 * jax.random.uniform(streams[3], (3, NSETS, K, 2, 1), jnp.float32)
    ripple_phase = 2.0 * math.pi * jax.random.uniform(streams[4], (3, NSETS, K, 2, 1), jnp.float32)
    ripple = jnp.sum(ripple_gain * jnp.cos(math.pi * ripple_freq * position + ripple_phase), axis=0)
    window = 1.0 + 0.6 * jnp.cos(math.pi * position)
    smooth_taps = window * (dc_level + ripple) / float(tap_count)
    sharp_gain = jnp.clip(jax.random.normal(streams[5], (3, NSETS, K, 2, 1), jnp.float32), -2.5, 2.5)
    sharp_freq = 2.0 * jax.random.uniform(streams[6], (3, NSETS, K, 2, 1), jnp.float32)
    sharp_phase = 2.0 * math.pi * jax.random.uniform(streams[7], (3, NSETS, K, 2, 1), jnp.float32)
    envelope = jnp.sum(sharp_gain * jnp.cos(math.pi * sharp_freq * position + sharp_phase), axis=0)
    sharp_taps = sign_flip * 0.8 * envelope / math.sqrt(float(tap_count))
    flat_draw = jnp.clip(jax.random.normal(streams[8], (NSETS, K, 2, tap_count), jnp.float32), -2.5, 2.5)
    flat_taps = 0.3 * flat_draw / math.sqrt(float(tap_count))
    return ((1.0 - sharpness) * smooth_taps + sharpness * sharp_taps + flat_taps).astype(jnp.float32)


def draw_row_taps(key, part):
    return kernel_taps(key, 11)


def draw_col_taps(key, part):
    return kernel_taps(key, 12)


def draw_mask(key, part):
    streams = jax.random.split(key, 5)
    strip_count = ROWS // TH
    rough_strip = (jax.random.permutation(streams[0], strip_count) % 2).astype(jnp.float32)
    strip_uniform = jax.random.uniform(streams[1], (strip_count,), jnp.float32)
    noise_level = rough_strip * (0.3 + 0.12 * strip_uniform) + (1.0 - rough_strip) * (0.02 + 0.03 * strip_uniform)
    row_level = jnp.repeat(noise_level, TH)[:, None]
    row_index = jnp.arange(ROWS, dtype=jnp.float32)[:, None]
    col_index = jnp.arange(TW, dtype=jnp.float32)[None, :]
    periods = 32.0 + 168.0 * jax.random.uniform(streams[2], (3,), jnp.float32)
    angular = 2.0 * math.pi / periods
    phases = 2.0 * math.pi * jax.random.uniform(streams[3], (3,), jnp.float32)
    smooth_field = 0.5 * jnp.sin(angular[0] * row_index + phases[0]) * jnp.cos(angular[1] * col_index + phases[1])
    smooth_field = smooth_field + 0.5 * jnp.sin(angular[2] * (row_index + col_index) + phases[2])
    pixel_noise = jnp.clip(0.6 * jax.random.normal(streams[4], (ROWS, TW), jnp.float32), -1.0, 1.0)
    return (0.5 + (0.45 - row_level) * smooth_field + row_level * pixel_noise).astype(jnp.float32)


def place_ends(entries, stream_key, low, high):
    shape = entries.shape
    place = [jax.random.randint(jax.random.fold_in(stream_key, axis), (), 0, shape[axis]) for axis in range(len(shape))]
    entries = entries.at[tuple(place)].set(low)
    longest = shape.index(max(shape))
    place[longest] = (place[longest] + 1) % shape[longest]
    return entries.at[tuple(place)].set(high)


def level_of(key, dims, shards, least, high):
    gain, own = 1.0, jax.random.fold_in(key, 6)
    for axis_at, blocks in shards:
        steps = jnp.exp(jax.random.uniform(jax.random.fold_in(own, axis_at), (blocks,), jnp.float32, least / len(shards), high / len(shards)))
        gain = gain * jnp.repeat(steps, dims[axis_at] // blocks).reshape([-1 if axis == axis_at else 1 for axis in range(len(dims))])
    return gain


def setup_inputs(seed: int = 0) -> dict:
    splits = jax.random.split(jax.random.key(seed), 9)
    mask = draw_mask(jax.random.fold_in(splits[8], 71), 0)
    target = place_ends((jax.random.randint(splits[1], (ROWS, TW), 0, 5) < 2).astype(jnp.int32), jax.random.fold_in(splits[1], 1), 0, 1)
    pixel_weight = draw_pixel_weight(jax.random.fold_in(splits[8], 71), 0)
    row_taps = draw_row_taps(jax.random.fold_in(splits[8], 71), 0)
    col_taps = draw_col_taps(jax.random.fold_in(splits[8], 71), 0)
    kernel_weights = draw_kernel_weights(jax.random.fold_in(splits[8], 71), 0)
    corner_set = place_ends(jax.random.randint(splits[6], (CORNERS,), 0, NSETS), jax.random.fold_in(splits[6], 1), 0, NSETS - 1).astype(jnp.int32)
    dose = jnp.clip(0.8 + 0.45 * jax.random.uniform(splits[7], (CORNERS,), jnp.float32) ** level_of(splits[7], (CORNERS,), ((0, 4),), -0.2, 0.2), 0.8, 1.25)
    return dict(mask=mask, target=target, pixel_weight=pixel_weight, row_taps=row_taps, col_taps=col_taps, kernel_weights=kernel_weights, corner_set=corner_set, dose=dose)


block_cols = 128
lse_sharp = 6.0
print_steep = 3.0
print_level = 1.0
step_rate = 0.25
small_eps = 1e-06

def toeplitz(tap_values, row_count):
    leading = tap_values.shape[:-1]
    span_width = row_count + tap_values.shape[-1] - 1
    padded = jnp.concatenate([tap_values, jnp.zeros(leading + (row_count,), tap_values.dtype)], axis=-1)
    repeated = jnp.tile(padded, (1,) * len(leading) + (row_count,))
    return repeated[..., :row_count * span_width].reshape(leading + (row_count, span_width))

def column_filter(masked, band_matrix):
    reach_cols = (band_matrix.shape[-1] - block_cols) // 2
    col_count = masked.shape[1]
    padded = jnp.pad(masked, ((0, 0), (reach_cols, reach_cols)))
    windows = jnp.stack([padded[:, b * block_cols:b * block_cols + block_cols + 2 * reach_cols] for b in range(col_count // block_cols)], axis=0)
    product = jnp.einsum('bri,poi->prbo', windows.astype(jnp.float32), band_matrix.astype(jnp.float32))
    return product.reshape(2, masked.shape[0], col_count)

def row_filter(band_matrix, cfield):
    product = jnp.einsum('aij,bjx->abix', band_matrix.astype(jnp.float32), cfield.astype(jnp.float32))
    return (product[0, 0] - product[1, 1], product[0, 1] + product[1, 0])

def row_adjoint(band_matrix, cotangent):
    product = jnp.einsum('aij,bix->abjx', band_matrix.astype(jnp.float32), cotangent.astype(jnp.float32))
    return jnp.stack([product[0, 0] + product[1, 1], product[0, 1] - product[1, 0]])

def column_adjoint(back_field, band_matrix):
    reach_cols = (band_matrix.shape[-1] - block_cols) // 2
    line_count = back_field.shape[1]
    col_count = back_field.shape[2]
    blocks = back_field.reshape(2, line_count, col_count // block_cols, block_cols)
    pieces = jnp.einsum('prbo,poi->bri', blocks.astype(jnp.float32), band_matrix.astype(jnp.float32))
    summed = jnp.zeros((line_count, col_count + 2 * reach_cols), jnp.float32)
    for b in range(col_count // block_cols):
        summed = summed.at[:, b * block_cols:b * block_cols + block_cols + 2 * reach_cols].add(pieces[b])
    return summed[:, reach_cols:reach_cols + col_count]

def corner_print(c, padded_rows, row_taps, col_taps, kernel_weights, corner_set, dose, target_value):
    set_index = corner_set[c]
    row_bands = toeplitz(row_taps[set_index].astype(jnp.bfloat16), TH)
    col_bands = toeplitz(col_taps[set_index].astype(jnp.bfloat16), block_cols)
    cfield = jax.vmap(column_filter, in_axes=(None, 0))(padded_rows, col_bands).astype(jnp.bfloat16)
    windows = jnp.stack([cfield[:, :, t * TH:t * TH + TH + 2 * R] for t in range(ROWS // TH)], axis=0)
    per_kernel = jax.vmap(row_filter, in_axes=(0, 0))
    field_real, field_imag = jax.vmap(per_kernel, in_axes=(None, 0))(row_bands, windows)
    weights = kernel_weights[set_index]
    intensity = dose[c] * lax.optimization_barrier(jnp.sum(weights[None, :, None, None] * (field_real * field_real + field_imag * field_imag), axis=1))
    intensity = intensity.reshape(ROWS, TW)
    printed = jax.nn.sigmoid(print_steep * (intensity - print_level))
    differ = printed - target_value
    exp_error = jnp.exp(lse_sharp * (differ * differ))
    return (row_bands, col_bands, field_real, field_imag, weights, printed, exp_error)

def reference(mask, target, pixel_weight, row_taps, col_taps, kernel_weights, corner_set, dose):
    masked = mask.astype(jnp.bfloat16)
    padded_rows = jnp.pad(masked, ((R, R), (0, 0)))
    target_value = target.astype(jnp.float32)
    corners = jnp.arange(CORNERS, dtype=jnp.int32)

    def first_pass(c):
        return corner_print(c, padded_rows, row_taps, col_taps, kernel_weights, corner_set, dose, target_value)[-1]
    exp_all = lax.map(first_pass, corners)
    denominator = lax.optimization_barrier(jnp.sum(exp_all, axis=0))
    soft_error = jnp.log(denominator) / lse_sharp

    def second_pass(running, c):
        row_bands, col_bands, field_real, field_imag, weights, printed, exp_error = corner_print(c, padded_rows, row_taps, col_taps, kernel_weights, corner_set, dose, target_value)
        slope = pixel_weight * (exp_error / denominator) * (2.0 * (printed - target_value)) * printed * (1.0 - printed) * print_steep
        factor = (2.0 * dose[c] * slope).reshape(ROWS // TH, TH, TW)
        fields = jnp.stack([field_real.astype(jnp.bfloat16), field_imag.astype(jnp.bfloat16)], axis=2)
        cotangent = (factor[:, None, None] * weights[None, :, None, None, None] * fields).astype(jnp.bfloat16)
        back_field = jax.vmap(jax.vmap(row_adjoint, in_axes=(0, 0)), in_axes=(None, 0))(row_bands, cotangent).astype(jnp.bfloat16)
        pieces = jax.vmap(jax.vmap(column_adjoint, in_axes=(0, 0)), in_axes=(0, None))(back_field, col_bands)
        tile_sums = lax.optimization_barrier(jnp.sum(pieces, axis=1))
        for t in range(ROWS // TH):
            running = running.at[t * TH:t * TH + TH + 2 * R].add(tile_sums[t])
        return (running, None)
    extended, _ = lax.scan(second_pass, jnp.zeros((ROWS + 2 * R, TW), jnp.float32), corners)
    gradient = extended[R:R + ROWS]
    root_mean = jnp.sqrt(jnp.sum(gradient * gradient) / (ROWS * TW) + small_eps)
    new_mask = jnp.clip(mask - step_rate / root_mean * gradient, 0.0, 1.0)
    return (soft_error, new_mask)
```

```python
import functools
import jax
import jax.numpy as jnp
from jax import lax
from jax.experimental import pallas as pl
from jax.experimental.pallas import tpu as pltpu
from jax.sharding import PartitionSpec as P

lse_sharp = 6.0
print_steep = 3.0
print_level = 1.0
step_rate = 0.25
small_eps = 1e-06
BLK = 128
F32 = jnp.float32
BF16 = jnp.bfloat16
MESH = pl.DeviceIdType.MESH


def kernel(
    n_t, n_c, mask_ref, target_ref, weight_ref, rt_ref, ct_ref, kw_ref, cs_ref, dose_ref,
    soft_ref, new_ref,
    xp, xw, tb, ra, cb, cf, fields, ssc, ssend, srecv, infosend, inforecv, fsend, frecv,
    softsend, softrecv, bkr, bkm, rimsend, rimrecv, gown, gsend, grecv, sqsend, sqrecv,
    sqtsend, sqtrecv,
    halo_s, halo_r, info_s, info_r, s_s, s_r, f_s, f_r, soft_s, soft_r, rim_s, rim_r,
    g_s, g_r, sq_s, sq_r, sqt_s, sqt_r,
):
    t = lax.axis_index("tile")
    z = lax.axis_index("corner")
    rows, cols = mask_ref.shape
    n_sets, n_k = kw_ref.shape
    taps = rt_ref.shape[-1]
    reach = (taps - 1) // 2
    ext = rows + 2 * reach
    win = BLK + 2 * reach
    n_b = cols // BLK
    share = rows // n_c
    per = n_sets * n_k // n_c
    local_corners = cs_ref.shape[0]
    s_me = (z * per) // n_k
    k_me = (z * per) % n_k

    def zpeer(d):
        return lax.rem(z + d, n_c)

    def tpeer(d):
        return lax.rem(t + d, n_t)

    def remote(src, dst, ssem, rsem, dev):
        return pltpu.make_async_remote_copy(
            src_ref=src, dst_ref=dst, send_sem=ssem, recv_sem=rsem,
            device_id=dev, device_id_type=MESH,
        )

    barrier = pltpu.get_barrier_semaphore()
    for d in range(1, n_c):
        pl.semaphore_signal(barrier, inc=1, device_id=(t, zpeer(d)), device_id_type=MESH)
    for d in range(1, n_t):
        pl.semaphore_signal(barrier, inc=1, device_id=(tpeer(d), z), device_id_type=MESH)

    padded = jnp.concatenate([mask_ref[...], jnp.zeros((rows, 2 * reach), F32)], axis=1)
    padded = pltpu.roll(padded, reach, 1)
    xp[reach : reach + rows, :] = padded.astype(BF16)

    @pl.when(t == 0)
    def _():
        xp[0:reach, :] = jnp.zeros((reach, cols + 2 * reach), BF16)
        rimrecv[1] = jnp.zeros((reach, cols), BF16)

    @pl.when(t == n_t - 1)
    def _():
        xp[reach + rows : ext, :] = jnp.zeros((reach, cols + 2 * reach), BF16)
        rimrecv[0] = jnp.zeros((reach, cols), BF16)

    for i in range(local_corners):
        infosend[2 * i : 2 * i + 1, :] = jnp.full((1, cols), cs_ref[i].astype(F32), F32)
        infosend[2 * i + 1 : 2 * i + 2, :] = jnp.full((1, cols), dose_ref[i], F32)
    inforecv[z] = infosend[...]

    pl.semaphore_wait(barrier, n_c - 1 + n_t - 1)

    down = remote(xp.at[pl.ds(rows, reach)], xp.at[pl.ds(0, reach)],
                  halo_s.at[0], halo_r.at[0], (tpeer(1), z))
    up = remote(xp.at[pl.ds(reach, reach)], xp.at[pl.ds(reach + rows, reach)],
                halo_s.at[1], halo_r.at[1], (tpeer(n_t - 1), z))

    @pl.when(t < n_t - 1)
    def _():
        down.start()

    @pl.when(t > 0)
    def _():
        up.start()

    infos = [
        remote(infosend, inforecv.at[z], info_s.at[d - 1], info_r.at[d - 1], (t, zpeer(d)))
        for d in range(1, n_c)
    ]
    for copy in infos:
        copy.start()

    tb[...] = jnp.zeros(tb.shape, F32)

    def tables(k, _):
        for p in range(2):
            tb[p : p + 1, 0:taps] = rt_ref[s_me, k_me + k, p : p + 1, :].astype(BF16).astype(F32)
            tb[2 + p : 3 + p, 0:taps] = ct_ref[s_me, k_me + k, p : p + 1, :].astype(BF16).astype(F32)

        def band(row, length, width):
            wide = jnp.broadcast_to(tb[row : row + 1, 0:width], (length, width))
            return pltpu.roll(wide, 0, 1, stride=1, stride_axis=0)

        re = band(0, rows, ext)
        im = band(1, rows, ext)
        ra[k, 0:rows, 0:ext] = re.astype(BF16)
        ra[k, rows : 2 * rows, ext : 2 * ext] = re.astype(BF16)
        ra[k, 0:rows, ext : 2 * ext] = (-im).astype(BF16)
        ra[k, rows : 2 * rows, 0:ext] = im.astype(BF16)
        base = pl.multiple_of(k * 2 * BLK, 2 * BLK)
        cb[pl.ds(base, BLK), :] = band(2, BLK, win).astype(BF16)
        cb[pl.ds(base + BLK, BLK), :] = band(3, BLK, win).astype(BF16)
        return 0

    lax.fori_loop(0, per, tables, 0)

    @pl.when(t > 0)
    def _():
        down.wait_recv()

    @pl.when(t < n_t - 1)
    def _():
        up.wait_recv()

    for b in range(n_b):
        xw[b * ext : (b + 1) * ext, :] = xp[:, b * BLK : b * BLK + win]
    ssc[...] = jnp.zeros(ssc.shape, F32)

    def forward(k, _):
        base = pl.multiple_of(k * 2 * BLK, 2 * BLK)
        c = lax.dot_general(
            xw[...], cb[pl.ds(base, 2 * BLK), :], (((1,), (1,)), ((), ())),
            preferred_element_type=F32,
        ).astype(BF16)
        for b in range(n_b):
            for p in range(2):
                cf[p * ext : (p + 1) * ext, b * BLK : (b + 1) * BLK] = c[
                    b * ext : (b + 1) * ext, p * BLK : (p + 1) * BLK
                ]
        field = jnp.dot(ra[k], cf[...], preferred_element_type=F32)
        re = field[0:rows]
        im = field[rows : 2 * rows]
        power = kw_ref[s_me, k_me + k] * (re * re + im * im)
        ssc[...] += power.reshape(ssc.shape)
        fields[k] = field.astype(BF16)
        return 0

    lax.fori_loop(0, per, forward, 0)

    ssend[...] = ssc[...].astype(BF16)
    scopies = [
        remote(ssend.at[zpeer(d)], srecv.at[z], s_s.at[d - 1], s_r.at[d - 1], (t, zpeer(d)))
        for d in range(1, n_c)
    ]
    for copy in scopies:
        copy.start()
    srecv[z] = ssend[z]
    for copy in infos:
        copy.wait_recv()
    for copy in scopies:
        copy.wait_recv()

    row0 = pl.multiple_of(z * share, share)
    owners = n_c // n_sets
    step = 16

    def pixels(j, _):
        r = pl.multiple_of(j * step, step)
        sums = []
        for s in range(n_sets):
            total = srecv[s * owners, pl.ds(r, step), :].astype(F32)
            for o in range(1, owners):
                total = total + srecv[s * owners + o, pl.ds(r, step), :].astype(F32)
            sums.append(total)
        goal = target_ref[pl.ds(row0 + r, step), :].astype(F32)
        pixel = weight_ref[pl.ds(row0 + r, step), :]
        for b in range(n_b):
            cut = slice(b * BLK, (b + 1) * BLK)
            den = jnp.zeros((step, BLK), F32)
            acc = [jnp.zeros((step, BLK), F32) for _ in range(n_sets)]
            tv = goal[:, cut]
            for c in range(n_c * local_corners):
                zc, i = divmod(c, local_corners)
                which = inforecv[zc, 2 * i : 2 * i + 1, cut]
                amount = inforecv[zc, 2 * i + 1 : 2 * i + 2, cut]
                which = jnp.broadcast_to(which, (step, BLK))
                chosen = sums[n_sets - 1][:, cut]
                for s in range(n_sets - 1):
                    chosen = jnp.where(which == float(s), sums[s][:, cut], chosen)
                printed = 1.0 / (1.0 + jnp.exp(print_steep * (print_level - amount * chosen)))
                differ = printed - tv
                err = jnp.exp(lse_sharp * (differ * differ))
                den = den + err
                part = amount * err * differ * (printed * (1.0 - printed))
                for s in range(n_sets):
                    acc[s] = acc[s] + jnp.where(which == float(s), part, 0.0)
            softsend[pl.ds(r, step), cut] = jnp.log(den) / lse_sharp
            scale = (4.0 * print_steep) * pixel[:, cut] / den
            for s in range(n_sets):
                fsend[s, pl.ds(r, step), cut] = (scale * acc[s]).astype(BF16)
        return 0

    lax.fori_loop(0, share // step, pixels, 0)

    fcopies = [
        remote(fsend.at[(zpeer(d) * per) // n_k], frecv.at[z], f_s.at[d - 1], f_r.at[d - 1],
               (t, zpeer(d)))
        for d in range(1, n_c)
    ]
    for copy in fcopies:
        copy.start()
    softs = [
        remote(softsend, softrecv.at[z], soft_s.at[d - 1], soft_r.at[d - 1], (t, zpeer(d)))
        for d in range(1, n_c)
    ]
    for copy in softs:
        copy.start()
    frecv[z] = fsend[s_me]
    softrecv[z] = softsend[...]
    for copy in fcopies:
        copy.wait_recv()

    def backward(k, _):
        factor = frecv[...].reshape(rows, cols).astype(F32) * kw_ref[s_me, k_me + k]
        both = jnp.concatenate([factor, factor], axis=0)
        cot = (both * fields[k].astype(F32)).astype(BF16)
        back = lax.dot_general(
            ra[k], cot, (((0,), (0,)), ((), ())), preferred_element_type=F32
        ).astype(BF16)
        for b in range(n_b):
            for p in range(2):
                piece = back[p * ext : (p + 1) * ext, b * BLK : (b + 1) * BLK]
                at = pl.ds(pl.multiple_of(k * 2 * BLK + p * BLK, BLK), BLK)
                low = b * 2 * reach
                bkr[low : low + reach, at] = piece[0:reach]
                bkr[low + reach : low + 2 * reach, at] = piece[reach + rows : ext]
                bkm[b * rows : (b + 1) * rows, at] = piece[reach : reach + rows]
        return 0

    lax.fori_loop(0, per, backward, 0)

    def column_sum(ref, count):
        g = jnp.dot(ref[...], cb[...], preferred_element_type=F32)
        strips = []
        for j in range(n_b + 1):
            value = None
            if j < n_b:
                value = g[j * count : (j + 1) * count, 0:BLK]
            if j > 0:
                other = g[(j - 1) * count : j * count, BLK : 2 * BLK]
                value = other if value is None else value + other
            strips.append(value)
        wide = jnp.concatenate(strips, axis=1)
        return pltpu.roll(wide, cols + reach, 1)[:, 0:cols]

    rim = column_sum(bkr, 2 * reach)
    rimsend[...] = rim.astype(BF16).reshape(rimsend.shape)
    rim_up = remote(rimsend.at[0], rimrecv.at[0], rim_s.at[0], rim_r.at[0], (tpeer(n_t - 1), z))
    rim_down = remote(rimsend.at[1], rimrecv.at[1], rim_s.at[1], rim_r.at[1], (tpeer(1), z))

    @pl.when(t > 0)
    def _():
        rim_up.start()

    @pl.when(t < n_t - 1)
    def _():
        rim_down.start()

    middle = column_sum(bkm, rows)

    @pl.when(t < n_t - 1)
    def _():
        rim_up.wait_recv()

    @pl.when(t > 0)
    def _():
        rim_down.wait_recv()

    rims = jnp.concatenate([rimrecv[1], rimrecv[0]], axis=0).astype(F32)
    if rows > 2 * reach:
        gap = jnp.zeros((rows - 2 * reach, cols), F32)
        rims = jnp.concatenate([rims[0:reach], gap, rims[reach:]], axis=0)
    gown[...] = (middle + rims).reshape(gown.shape)
    gsend[...] = gown[...].astype(BF16)
    gcopies = [
        remote(gsend.at[zpeer(d)], grecv.at[d - 1], g_s.at[d - 1], g_r.at[d - 1], (t, zpeer(d)))
        for d in range(1, n_c)
    ]
    for copy in gcopies:
        copy.start()
    for copy in softs:
        copy.wait_recv()
    soft_ref[...] = softrecv[...].reshape(rows, cols)
    grad = gown[z]
    for d in range(1, n_c):
        gcopies[d - 1].wait_recv()
        grad = grad + grecv[d - 1].astype(F32)

    square = jnp.sum((grad * grad).reshape(share // 8, 8, cols), axis=0)
    part = square[:, 0:BLK]
    for b in range(1, n_b):
        part = part + square[:, b * BLK : (b + 1) * BLK]
    sqsend[...] = part
    sqz = [
        remote(sqsend, sqrecv.at[d - 1], sq_s.at[d - 1], sq_r.at[d - 1], (t, zpeer(d)))
        for d in range(1, n_c)
    ]
    for copy in sqz:
        copy.start()
    for d in range(1, n_c):
        sqz[d - 1].wait_recv()
        part = part + sqrecv[d - 1]
    sqtsend[...] = part
    sqt = [
        remote(sqtsend, sqtrecv.at[d - 1], sqt_s.at[d - 1], sqt_r.at[d - 1], (tpeer(d), z))
        for d in range(1, n_t)
    ]
    for copy in sqt:
        copy.start()
    for d in range(1, n_t):
        sqt[d - 1].wait_recv()
        part = part + sqtrecv[d - 1]
    total = jnp.sum(jnp.sum(part, axis=0, keepdims=True), axis=1, keepdims=True)
    rate = step_rate / jnp.sqrt(total / (rows * n_t * cols) + small_eps)
    own = mask_ref[pl.ds(row0, share), :]
    new_ref[...] = jnp.clip(own - rate * grad, 0.0, 1.0)

    @pl.when(t < n_t - 1)
    def _():
        down.wait_send()
        rim_down.wait_send()

    @pl.when(t > 0)
    def _():
        up.wait_send()
        rim_up.wait_send()

    for copy in infos + scopies + fcopies + softs + gcopies + sqz + sqt:
        copy.wait_send()


def solution(mesh):
    n_t, n_c = mesh.shape["tile"], mesh.shape["corner"]

    def local(mask, target, pixel_weight, row_taps, col_taps, kernel_weights, corner_set, dose):
        rows, cols = mask.shape
        n_sets, n_k, _, taps = row_taps.shape
        reach = (taps - 1) // 2
        ext, win, n_b = rows + 2 * reach, BLK + 2 * reach, cols // BLK
        share = rows // n_c
        per = n_sets * n_k // n_c
        info_rows = 8 * ((2 * corner_set.shape[0] + 7) // 8)
        vmem = pl.BlockSpec(memory_space=pltpu.VMEM)
        smem = pl.BlockSpec(memory_space=pltpu.SMEM)
        V = pltpu.VMEM
        dma = pltpu.SemaphoreType.DMA
        zc = dma((n_c - 1,))
        scratch = [
            V((ext, cols + 2 * reach), BF16),
            V((n_b * ext, win), BF16),
            V((8, max(ext, win)), F32),
            V((per, 2 * rows, 2 * ext), BF16),
            V((per * 2 * BLK, win), BF16),
            V((2 * ext, cols), BF16),
            V((per, 2 * rows, cols), BF16),
            V((n_c, share, cols), F32),
            V((n_c, share, cols), BF16),
            V((n_c, share, cols), BF16),
            V((info_rows, cols), F32),
            V((n_c, info_rows, cols), F32),
            V((n_sets, share, cols), BF16),
            V((n_c, share, cols), BF16),
            V((share, cols), F32),
            V((n_c, share, cols), F32),
            V((n_b * 2 * reach, per * 2 * BLK), BF16),
            V((n_b * rows, per * 2 * BLK), BF16),
            V((2, reach, cols), BF16),
            V((2, reach, cols), BF16),
            V((n_c, share, cols), F32),
            V((n_c, share, cols), BF16),
            V((n_c - 1, share, cols), BF16),
            V((8, BLK), F32),
            V((n_c - 1, 8, BLK), F32),
            V((8, BLK), F32),
            V((n_t - 1, 8, BLK), F32),
            dma((2,)), dma((2,)),
            zc, zc, zc, zc, zc, zc, zc, zc,
            dma((2,)), dma((2,)),
            zc, zc, zc, zc,
            dma((n_t - 1,)), dma((n_t - 1,)),
        ]
        return pl.pallas_call(
            functools.partial(kernel, n_t, n_c),
            out_shape=(
                jax.ShapeDtypeStruct((rows, cols), F32),
                jax.ShapeDtypeStruct((share, cols), F32),
            ),
            in_specs=[vmem] * 5 + [smem] * 3,
            out_specs=(vmem, vmem),
            scratch_shapes=scratch,
            compiler_params=pltpu.CompilerParams(
                collective_id=0, has_side_effects=True, vmem_limit_bytes=44 * 1024 * 1024
            ),
        )(mask, target, pixel_weight, row_taps, col_taps, kernel_weights, corner_set, dose)

    placed = (
        P("tile", None),
        P("tile", None),
        P("tile", None),
        P(),
        P(),
        P(),
        P("corner"),
        P("corner"),
    )
    return jax.shard_map(
        local,
        mesh=mesh,
        in_specs=placed,
        out_specs=(P("tile", None), P(("tile", "corner"), None)),
        check_vma=False,
    )
```

```python
import functools
import jax
import jax.numpy as jnp
from jax import lax
from jax.experimental import pallas as pl
from jax.experimental.pallas import tpu as pltpu
from jax.sharding import PartitionSpec as P

lse_sharp = 6.0
print_steep = 3.0
print_level = 1.0
step_rate = 0.25
small_eps = 1e-06
BLK = 128
F32 = jnp.float32
BF16 = jnp.bfloat16
MESH = pl.DeviceIdType.MESH


def kernel(
    n_t, n_c, mask_hbm, target_hbm, weight_hbm, rt_hbm, ct_hbm, kw_hbm, cs_hbm, dose_hbm,
    soft_ref, new_ref,
    mask_ref, target_ref, weight_ref, rt_ref, ct_ref, kw_ref, cs_ref, dose_ref, in_s,
    xp, xw, tb, ra, cb, cbt, cf, fields, ssc, ssend, srecv, infosend, inforecv, fsend, frecv,
    softsend, softrecv, bkr, bkm, rimsend, rimrecv, gown, gsend, grecv, sqsend, sqrecv,
    halo_s, halo_r, info_s, info_r, s_s, s_r, f_s, f_r, soft_s, soft_r, rim_s, rim_r,
    g_s, g_r, sq_s, sq_r,
):
    t = lax.axis_index("tile")
    z = lax.axis_index("corner")
    rows, cols = mask_ref.shape
    n_sets, n_k = kw_ref.shape
    taps = rt_ref.shape[-1]
    reach = (taps - 1) // 2
    ext = rows + 2 * reach
    win = BLK + 2 * reach
    n_b = cols // BLK
    share = rows // n_c
    per = n_sets * n_k // n_c
    local_corners = cs_ref.shape[0]
    s_me = (z * per) // n_k
    k_me = (z * per) % n_k

    def zpeer(d):
        return lax.rem(z + d, n_c)

    def tpeer(d):
        return lax.rem(t + d, n_t)

    def remote(src, dst, ssem, rsem, dev):
        return pltpu.make_async_remote_copy(
            src_ref=src, dst_ref=dst, send_sem=ssem, recv_sem=rsem,
            device_id=dev, device_id_type=MESH,
        )

    barrier = pltpu.get_barrier_semaphore()
    everyone = n_t * n_c

    def anyone(d):
        other = lax.rem(t * n_c + z + d, everyone)
        return (other // n_c, lax.rem(other, n_c))

    def greet(d, _):
        pl.semaphore_signal(barrier, inc=1, device_id=anyone(d), device_id_type=MESH)
        return 0

    lax.fori_loop(1, everyone, greet, 0)

    row0 = pl.multiple_of(z * share, share)
    loads = [
        pltpu.make_async_copy(src, dst, in_s.at[i])
        for i, (src, dst) in enumerate([
            (mask_hbm, mask_ref),
            (cs_hbm, cs_ref),
            (dose_hbm, dose_ref),
            (rt_hbm.at[s_me], rt_ref),
            (ct_hbm.at[s_me], ct_ref),
            (kw_hbm, kw_ref),
            (target_hbm.at[pl.ds(row0, share)], target_ref),
            (weight_hbm.at[pl.ds(row0, share)], weight_ref),
        ])
    ]
    for load in loads:
        load.start()
    loads[0].wait()

    padded = jnp.concatenate([mask_ref[...], jnp.zeros((rows, 2 * reach), F32)], axis=1)
    padded = pltpu.roll(padded, reach, 1)
    xp[reach : reach + rows, :] = padded.astype(BF16)

    @pl.when(t == 0)
    def _():
        xp[0:reach, :] = jnp.zeros((reach, cols + 2 * reach), BF16)
        rimrecv[1] = jnp.zeros((reach, cols), BF16)

    @pl.when(t == n_t - 1)
    def _():
        xp[reach + rows : ext, :] = jnp.zeros((reach, cols + 2 * reach), BF16)
        rimrecv[0] = jnp.zeros((reach, cols), BF16)

    loads[1].wait()
    loads[2].wait()
    for i in range(local_corners):
        infosend[2 * i : 2 * i + 1, :] = jnp.full((1, cols), cs_ref[i].astype(F32), F32)
        infosend[2 * i + 1 : 2 * i + 2, :] = jnp.full((1, cols), dose_ref[i], F32)
    inforecv[z] = infosend[...]

    tb[...] = jnp.zeros(tb.shape, F32)

    loads[3].wait()
    loads[4].wait()

    def tables(k, _):
        for p in range(2):
            tb[p : p + 1, 0:taps] = rt_ref[k_me + k, p : p + 1, :].astype(BF16).astype(F32)
            tb[2 + p : 3 + p, 0:taps] = ct_ref[k_me + k, p : p + 1, :].astype(BF16).astype(F32)

        def band(row, length, width):
            wide = jnp.broadcast_to(tb[row : row + 1, 0:width], (length, width))
            return pltpu.roll(wide, 0, 1, stride=1, stride_axis=0)

        re = band(0, rows, ext)
        im = band(1, rows, ext)
        ra[k, 0:rows, 0:ext] = re.astype(BF16)
        ra[k, rows : 2 * rows, ext : 2 * ext] = re.astype(BF16)
        ra[k, 0:rows, ext : 2 * ext] = (-im).astype(BF16)
        ra[k, rows : 2 * rows, 0:ext] = im.astype(BF16)
        base = pl.multiple_of(k * 2 * BLK, 2 * BLK)
        pair = jnp.concatenate([band(2, BLK, win), band(3, BLK, win)], axis=0)
        cb[pl.ds(base, 2 * BLK), :] = pair.astype(BF16)
        cbt[k] = pair.T.astype(BF16)
        return 0

    lax.fori_loop(0, per, tables, 0)

    pl.semaphore_wait(barrier, everyone - 1)

    down = remote(xp.at[pl.ds(rows, reach)], xp.at[pl.ds(0, reach)],
                  halo_s.at[0], halo_r.at[0], (tpeer(1), z))
    up = remote(xp.at[pl.ds(reach, reach)], xp.at[pl.ds(reach + rows, reach)],
                halo_s.at[1], halo_r.at[1], (tpeer(n_t - 1), z))

    @pl.when(t < n_t - 1)
    def _():
        down.start()

    @pl.when(t > 0)
    def _():
        up.start()

    infos = [
        remote(infosend, inforecv.at[z], info_s.at[d - 1], info_r.at[d - 1], (t, zpeer(d)))
        for d in range(1, n_c)
    ]
    for copy in infos:
        copy.start()

    for b in range(n_b):
        xw[b * rows : (b + 1) * rows, :] = xp[reach : reach + rows, b * BLK : b * BLK + win]

    def middle_columns(k, _):
        c = jnp.dot(xw[0 : n_b * rows, :], cbt[k], preferred_element_type=F32).astype(BF16)
        for b in range(n_b):
            for p in range(2):
                low = p * ext + reach
                cf[k, low : low + rows, b * BLK : (b + 1) * BLK] = c[
                    b * rows : (b + 1) * rows, p * BLK : (p + 1) * BLK
                ]
        return 0

    lax.fori_loop(0, per, middle_columns, 0)

    @pl.when(t > 0)
    def _():
        down.wait_recv()

    @pl.when(t < n_t - 1)
    def _():
        up.wait_recv()

    side = n_b * rows
    for b in range(n_b):
        low = side + b * 2 * reach
        cut = slice(b * BLK, b * BLK + win)
        xw[low : low + reach, :] = xp[0:reach, cut]
        xw[low + reach : low + 2 * reach, :] = xp[reach + rows : ext, cut]
    ssc[...] = jnp.zeros(ssc.shape, F32)
    for load in loads[5:]:
        load.wait()

    def rim_columns(k, _):
        c = jnp.dot(xw[side:, :], cbt[k], preferred_element_type=F32).astype(BF16)
        for b in range(n_b):
            for p in range(2):
                piece = c[b * 2 * reach : (b + 1) * 2 * reach, p * BLK : (p + 1) * BLK]
                out = slice(b * BLK, (b + 1) * BLK)
                cf[k, p * ext : p * ext + reach, out] = piece[0:reach]
                cf[k, p * ext + reach + rows : (p + 1) * ext, out] = piece[reach:]
        return 0

    lax.fori_loop(0, per, rim_columns, 0)

    def forward(k, _):
        field = jnp.dot(ra[k], cf[k], preferred_element_type=F32)
        re = field[0:rows]
        im = field[rows : 2 * rows]
        power = kw_ref[s_me, k_me + k] * (re * re + im * im)
        ssc[...] += power.reshape(ssc.shape)
        fields[k] = field.astype(BF16)
        return 0

    lax.fori_loop(0, per, forward, 0)

    ssend[...] = ssc[...].astype(BF16)
    scopies = [
        remote(ssend.at[zpeer(d)], srecv.at[z], s_s.at[d - 1], s_r.at[d - 1], (t, zpeer(d)))
        for d in range(1, n_c)
    ]
    for copy in scopies:
        copy.start()
    srecv[z] = ssend[z]
    for copy in infos:
        copy.wait_recv()
    for copy in scopies:
        copy.wait_recv()

    owners = n_c // n_sets
    step = 16

    def pixels(j, _):
        r = pl.multiple_of(j * step, step)
        sums = []
        for s in range(n_sets):
            total = srecv[s * owners, pl.ds(r, step), :].astype(F32)
            for o in range(1, owners):
                total = total + srecv[s * owners + o, pl.ds(r, step), :].astype(F32)
            sums.append(total)
        goal = target_ref[pl.ds(r, step), :].astype(F32)
        pixel = weight_ref[pl.ds(r, step), :]
        for b in range(n_b):
            cut = slice(b * BLK, (b + 1) * BLK)
            den = jnp.zeros((step, BLK), F32)
            acc = [jnp.zeros((step, BLK), F32) for _ in range(n_sets)]
            tv = goal[:, cut]
            for c in range(n_c * local_corners):
                zc, i = divmod(c, local_corners)
                which = inforecv[zc, 2 * i : 2 * i + 1, cut]
                amount = inforecv[zc, 2 * i + 1 : 2 * i + 2, cut]
                which = jnp.broadcast_to(which, (step, BLK))
                chosen = sums[n_sets - 1][:, cut]
                for s in range(n_sets - 1):
                    chosen = jnp.where(which == float(s), sums[s][:, cut], chosen)
                printed = 1.0 / (1.0 + jnp.exp(print_steep * (print_level - amount * chosen)))
                differ = printed - tv
                err = jnp.exp(lse_sharp * (differ * differ))
                den = den + err
                part = amount * err * differ * (printed * (1.0 - printed))
                for s in range(n_sets):
                    acc[s] = acc[s] + jnp.where(which == float(s), part, 0.0)
            softsend[pl.ds(r, step), cut] = jnp.log(den) / lse_sharp
            scale = (4.0 * print_steep) * pixel[:, cut] / den
            for s in range(n_sets):
                fsend[s, pl.ds(r, step), cut] = (scale * acc[s]).astype(BF16)
        return 0

    lax.fori_loop(0, share // step, pixels, 0)

    fcopies = [
        remote(fsend.at[(zpeer(d) * per) // n_k], frecv.at[z], f_s.at[d - 1], f_r.at[d - 1],
               (t, zpeer(d)))
        for d in range(1, n_c)
    ]
    for copy in fcopies:
        copy.start()
    softs = [
        remote(softsend, softrecv.at[z], soft_s.at[d - 1], soft_r.at[d - 1], (t, zpeer(d)))
        for d in range(1, n_c)
    ]
    frecv[z] = fsend[s_me]
    softrecv[z] = softsend[...]
    for copy in fcopies:
        copy.wait_recv()
    for copy in softs:
        copy.start()

    def backward(k, _):
        factor = frecv[...].reshape(rows, cols).astype(F32) * kw_ref[s_me, k_me + k]
        both = jnp.concatenate([factor, factor], axis=0)
        cot = (both * fields[k].astype(F32)).astype(BF16)
        back = lax.dot_general(
            ra[k], cot, (((0,), (0,)), ((), ())), preferred_element_type=F32
        ).astype(BF16)
        for b in range(n_b):
            for p in range(2):
                piece = back[p * ext : (p + 1) * ext, b * BLK : (b + 1) * BLK]
                at = pl.ds(pl.multiple_of(k * 2 * BLK + p * BLK, BLK), BLK)
                low = b * 2 * reach
                bkr[low : low + reach, at] = piece[0:reach]
                bkr[low + reach : low + 2 * reach, at] = piece[reach + rows : ext]
                bkm[b * rows : (b + 1) * rows, at] = piece[reach : reach + rows]
        return 0

    lax.fori_loop(0, per, backward, 0)

    def column_sum(ref, count):
        g = jnp.dot(ref[...], cb[...], preferred_element_type=F32)
        strips = []
        for j in range(n_b + 1):
            value = None
            if j < n_b:
                value = g[j * count : (j + 1) * count, 0:BLK]
            if j > 0:
                other = g[(j - 1) * count : j * count, BLK : 2 * BLK]
                value = other if value is None else value + other
            strips.append(value)
        wide = jnp.concatenate(strips, axis=1)
        return pltpu.roll(wide, cols + reach, 1)[:, 0:cols]

    rim = column_sum(bkr, 2 * reach)
    rimsend[...] = rim.astype(BF16).reshape(rimsend.shape)
    rim_up = remote(rimsend.at[0], rimrecv.at[0], rim_s.at[0], rim_r.at[0], (tpeer(n_t - 1), z))
    rim_down = remote(rimsend.at[1], rimrecv.at[1], rim_s.at[1], rim_r.at[1], (tpeer(1), z))

    @pl.when(t > 0)
    def _():
        rim_up.start()

    @pl.when(t < n_t - 1)
    def _():
        rim_down.start()

    middle = column_sum(bkm, rows)

    @pl.when(t < n_t - 1)
    def _():
        rim_up.wait_recv()

    @pl.when(t > 0)
    def _():
        rim_down.wait_recv()

    rims = jnp.concatenate([rimrecv[1], rimrecv[0]], axis=0).astype(F32)
    if rows > 2 * reach:
        gap = jnp.zeros((rows - 2 * reach, cols), F32)
        rims = jnp.concatenate([rims[0:reach], gap, rims[reach:]], axis=0)
    gown[...] = (middle + rims).reshape(gown.shape)
    gsend[...] = gown[...].astype(BF16)
    gcopies = [
        remote(gsend.at[zpeer(d)], grecv.at[d - 1], g_s.at[d - 1], g_r.at[d - 1], (t, zpeer(d)))
        for d in range(1, n_c)
    ]
    for copy in gcopies:
        copy.start()
    for copy in softs:
        copy.wait_recv()
    soft_ref[...] = softrecv[...].reshape(rows, cols)
    grad = gown[z]
    for d in range(1, n_c):
        gcopies[d - 1].wait_recv()
        grad = grad + grecv[d - 1].astype(F32)

    square = jnp.sum((grad * grad).reshape(share // 8, 8, cols), axis=0)
    part = square[:, 0:BLK]
    for b in range(1, n_b):
        part = part + square[:, b * BLK : (b + 1) * BLK]
    sqsend[...] = jnp.sum(part, axis=0, keepdims=True)

    def square_copy(d):
        return remote(sqsend, sqrecv.at[d - 1], sq_s.at[d - 1], sq_r.at[d - 1], anyone(d))

    def square_start(d, _):
        square_copy(d).start()
        return 0

    def square_wait(d, _):
        square_copy(d).wait_recv()
        return 0

    lax.fori_loop(1, everyone, square_start, 0)
    lax.fori_loop(1, everyone, square_wait, 0)
    part = sqsend[...] + jnp.sum(sqrecv[...], axis=0)
    total = jnp.sum(part, axis=1, keepdims=True)
    rate = step_rate / jnp.sqrt(total / (rows * n_t * cols) + small_eps)
    own = mask_ref[pl.ds(row0, share), :]
    new_ref[...] = jnp.clip(own - rate * grad, 0.0, 1.0)

    @pl.when(t < n_t - 1)
    def _():
        down.wait_send()
        rim_down.wait_send()

    @pl.when(t > 0)
    def _():
        up.wait_send()
        rim_up.wait_send()

    for copy in infos + scopies + fcopies + softs + gcopies:
        copy.wait_send()

    def square_sent(d, _):
        square_copy(d).wait_send()
        return 0

    lax.fori_loop(1, everyone, square_sent, 0)


def solution(mesh):
    n_t, n_c = mesh.shape["tile"], mesh.shape["corner"]

    def local(mask, target, pixel_weight, row_taps, col_taps, kernel_weights, corner_set, dose):
        rows, cols = mask.shape
        n_sets, n_k, _, taps = row_taps.shape
        reach = (taps - 1) // 2
        ext, win, n_b = rows + 2 * reach, BLK + 2 * reach, cols // BLK
        share = rows // n_c
        per = n_sets * n_k // n_c
        info_rows = 8 * ((2 * corner_set.shape[0] + 7) // 8)
        vmem = pl.BlockSpec(memory_space=pltpu.VMEM)
        hbm = pl.BlockSpec(memory_space=pl.ANY)
        S = pltpu.SMEM
        V = pltpu.VMEM
        dma = pltpu.SemaphoreType.DMA
        zc = dma((n_c - 1,))
        scratch = [
            V((rows, cols), F32),
            V((share, cols), jnp.int32),
            V((share, cols), F32),
            V((n_k, 2, taps), F32),
            V((n_k, 2, taps), F32),
            S((n_sets, n_k), F32),
            S(corner_set.shape, jnp.int32),
            S(dose.shape, F32),
            dma((8,)),
            V((ext, cols + 2 * reach), BF16),
            V((n_b * ext, win), BF16),
            V((8, max(ext, win)), F32),
            V((per, 2 * rows, 2 * ext), BF16),
            V((per * 2 * BLK, win), BF16),
            V((per, win, 2 * BLK), BF16),
            V((per, 2 * ext, cols), BF16),
            V((per, 2 * rows, cols), BF16),
            V((n_c, share, cols), F32),
            V((n_c, share, cols), BF16),
            V((n_c, share, cols), BF16),
            V((info_rows, cols), F32),
            V((n_c, info_rows, cols), F32),
            V((n_sets, share, cols), BF16),
            V((n_c, share, cols), BF16),
            V((share, cols), F32),
            V((n_c, share, cols), F32),
            V((n_b * 2 * reach, per * 2 * BLK), BF16),
            V((n_b * rows, per * 2 * BLK), BF16),
            V((2, reach, cols), BF16),
            V((2, reach, cols), BF16),
            V((n_c, share, cols), F32),
            V((n_c, share, cols), BF16),
            V((n_c - 1, share, cols), BF16),
            V((1, BLK), F32),
            V((n_t * n_c - 1, 1, BLK), F32),
            dma((2,)), dma((2,)),
            zc, zc, zc, zc, zc, zc, zc, zc,
            dma((2,)), dma((2,)),
            zc, zc,
            dma((n_t * n_c - 1,)), dma((n_t * n_c - 1,)),
        ]
        return pl.pallas_call(
            functools.partial(kernel, n_t, n_c),
            out_shape=(
                jax.ShapeDtypeStruct((rows, cols), F32),
                jax.ShapeDtypeStruct((share, cols), F32),
            ),
            in_specs=[hbm] * 8,
            out_specs=(vmem, vmem),
            scratch_shapes=scratch,
            compiler_params=pltpu.CompilerParams(
                collective_id=0, has_side_effects=True, vmem_limit_bytes=60 * 1024 * 1024
            ),
        )(mask, target, pixel_weight, row_taps, col_taps, kernel_weights, corner_set, dose)

    placed = (
        P("tile", None),
        P("tile", None),
        P("tile", None),
        P(),
        P(),
        P(),
        P("corner"),
        P("corner"),
    )
    return jax.shard_map(
        local,
        mesh=mesh,
        in_specs=placed,
        out_specs=(P("tile", None), P(("tile", "corner"), None)),
        check_vma=False,
    )
```

```python
import functools
import jax
import jax.numpy as jnp
from jax import lax
from jax.experimental import pallas as pl
from jax.experimental.pallas import tpu as pltpu
from jax.sharding import PartitionSpec as P

lse_sharp = 6.0
print_steep = 3.0
print_level = 1.0
step_rate = 0.25
small_eps = 1e-06
BLK = 128
F32 = jnp.float32
BF16 = jnp.bfloat16
MESH = pl.DeviceIdType.MESH


def kernel(
    n_t, n_c, mask_hbm, target_hbm, weight_hbm, rt_hbm, ct_hbm, kw_hbm, cs_hbm, dose_hbm,
    soft_ref, new_ref,
    mask_ref, target_ref, weight_ref, rt_ref, ct_ref, kw_ref, cs_ref, dose_ref, in_s,
    xp, xw, tb, ra, cb, cbt, cf, fields, ssc, ssend, srecv, infosend, inforecv, fsend, frecv,
    softsend, softrecv, bkr, bkm, rimsend, rimrecv, gown, gsend, grecv, sqsend, sqrecv,
    halo_s, halo_r, info_s, info_r, s_s, s_r, f_s, f_r, soft_s, soft_r, rim_s, rim_r,
    g_s, g_r, sq_s, sq_r,
):
    t = lax.axis_index("tile")
    z = lax.axis_index("corner")
    rows, cols = mask_ref.shape
    n_sets, n_k = kw_ref.shape
    taps = rt_ref.shape[-1]
    reach = (taps - 1) // 2
    ext = rows + 2 * reach
    win = BLK + 2 * reach
    n_b = cols // BLK
    share = rows // n_c
    per = n_sets * n_k // n_c
    local_corners = cs_ref.shape[0]
    s_me = (z * per) // n_k
    k_me = (z * per) % n_k

    def zpeer(d):
        return lax.rem(z + d, n_c)

    def tpeer(d):
        return lax.rem(t + d, n_t)

    def remote(src, dst, ssem, rsem, dev):
        return pltpu.make_async_remote_copy(
            src_ref=src, dst_ref=dst, send_sem=ssem, recv_sem=rsem,
            device_id=dev, device_id_type=MESH,
        )

    barrier = pltpu.get_barrier_semaphore()
    everyone = n_t * n_c

    def anyone(d):
        other = lax.rem(t * n_c + z + d, everyone)
        return (other // n_c, lax.rem(other, n_c))

    def greet(d, _):
        pl.semaphore_signal(barrier, inc=1, device_id=anyone(d), device_id_type=MESH)
        return 0

    lax.fori_loop(1, everyone, greet, 0, unroll=4)

    row0 = pl.multiple_of(z * share, share)
    loads = [
        pltpu.make_async_copy(src, dst, in_s.at[i])
        for i, (src, dst) in enumerate([
            (mask_hbm, mask_ref),
            (cs_hbm, cs_ref),
            (dose_hbm, dose_ref),
            (rt_hbm.at[s_me], rt_ref),
            (ct_hbm.at[s_me], ct_ref),
            (kw_hbm, kw_ref),
            (target_hbm.at[pl.ds(row0, share)], target_ref),
            (weight_hbm.at[pl.ds(row0, share)], weight_ref),
        ])
    ]
    for load in loads:
        load.start()
    loads[0].wait()

    padded = jnp.concatenate([mask_ref[...], jnp.zeros((rows, 2 * reach), F32)], axis=1)
    padded = pltpu.roll(padded, reach, 1)
    xp[reach : reach + rows, :] = padded.astype(BF16)

    @pl.when(t == 0)
    def _():
        xp[0:reach, :] = jnp.zeros((reach, cols + 2 * reach), BF16)
        rimrecv[1] = jnp.zeros((reach, cols), BF16)

    @pl.when(t == n_t - 1)
    def _():
        xp[reach + rows : ext, :] = jnp.zeros((reach, cols + 2 * reach), BF16)
        rimrecv[0] = jnp.zeros((reach, cols), BF16)

    loads[1].wait()
    loads[2].wait()
    for i in range(local_corners):
        infosend[2 * i : 2 * i + 1, :] = jnp.full((1, cols), cs_ref[i].astype(F32), F32)
        infosend[2 * i + 1 : 2 * i + 2, :] = jnp.full((1, cols), dose_ref[i], F32)
    inforecv[z] = infosend[...]

    tb[...] = jnp.zeros(tb.shape, F32)

    loads[3].wait()
    loads[4].wait()

    def tables(k, _):
        for p in range(2):
            tb[p : p + 1, 0:taps] = rt_ref[k_me + k, p : p + 1, :].astype(BF16).astype(F32)
            tb[2 + p : 3 + p, 0:taps] = ct_ref[k_me + k, p : p + 1, :].astype(BF16).astype(F32)

        def band(row, length, width):
            wide = jnp.broadcast_to(tb[row : row + 1, 0:width], (length, width))
            return pltpu.roll(wide, 0, 1, stride=1, stride_axis=0)

        re = band(0, rows, ext)
        im = band(1, rows, ext)
        ra[k, 0:rows, 0:ext] = re.astype(BF16)
        ra[k, rows : 2 * rows, ext : 2 * ext] = re.astype(BF16)
        ra[k, 0:rows, ext : 2 * ext] = (-im).astype(BF16)
        ra[k, rows : 2 * rows, 0:ext] = im.astype(BF16)
        base = pl.multiple_of(k * 2 * BLK, 2 * BLK)
        pair = jnp.concatenate([band(2, BLK, win), band(3, BLK, win)], axis=0)
        cb[pl.ds(base, 2 * BLK), :] = pair.astype(BF16)
        cbt[k] = pair.T.astype(BF16)
        return 0

    lax.fori_loop(0, per, tables, 0)

    pl.semaphore_wait(barrier, everyone - 1)

    down = remote(xp.at[pl.ds(rows, reach)], xp.at[pl.ds(0, reach)],
                  halo_s.at[0], halo_r.at[0], (tpeer(1), z))
    up = remote(xp.at[pl.ds(reach, reach)], xp.at[pl.ds(reach + rows, reach)],
                halo_s.at[1], halo_r.at[1], (tpeer(n_t - 1), z))

    @pl.when(t < n_t - 1)
    def _():
        down.start()

    @pl.when(t > 0)
    def _():
        up.start()

    infos = [
        remote(infosend, inforecv.at[z], info_s.at[d - 1], info_r.at[d - 1], (t, zpeer(d)))
        for d in range(1, n_c)
    ]
    for copy in infos:
        copy.start()

    for b in range(n_b):
        xw[b * rows : (b + 1) * rows, :] = xp[reach : reach + rows, b * BLK : b * BLK + win]

    def middle_columns(k, _):
        c = jnp.dot(xw[0 : n_b * rows, :], cbt[k], preferred_element_type=F32).astype(BF16)
        for b in range(n_b):
            for p in range(2):
                low = p * ext + reach
                cf[k, low : low + rows, b * BLK : (b + 1) * BLK] = c[
                    b * rows : (b + 1) * rows, p * BLK : (p + 1) * BLK
                ]
        return 0

    lax.fori_loop(0, per, middle_columns, 0, unroll=True)

    @pl.when(t > 0)
    def _():
        down.wait_recv()

    @pl.when(t < n_t - 1)
    def _():
        up.wait_recv()

    side = n_b * rows
    for b in range(n_b):
        low = side + b * 2 * reach
        cut = slice(b * BLK, b * BLK + win)
        xw[low : low + reach, :] = xp[0:reach, cut]
        xw[low + reach : low + 2 * reach, :] = xp[reach + rows : ext, cut]
    ssc[...] = jnp.zeros(ssc.shape, F32)
    for load in loads[5:]:
        load.wait()

    def rim_columns(k, _):
        c = jnp.dot(xw[side:, :], cbt[k], preferred_element_type=F32).astype(BF16)
        for b in range(n_b):
            for p in range(2):
                piece = c[b * 2 * reach : (b + 1) * 2 * reach, p * BLK : (p + 1) * BLK]
                out = slice(b * BLK, (b + 1) * BLK)
                cf[k, p * ext : p * ext + reach, out] = piece[0:reach]
                cf[k, p * ext + reach + rows : (p + 1) * ext, out] = piece[reach:]
        return 0

    lax.fori_loop(0, per, rim_columns, 0, unroll=True)

    def forward(k, _):
        field = jnp.dot(ra[k], cf[k], preferred_element_type=F32)
        re = field[0:rows]
        im = field[rows : 2 * rows]
        power = kw_ref[s_me, k_me + k] * (re * re + im * im)
        ssc[...] += power.reshape(ssc.shape)
        fields[k] = field.astype(BF16)
        return 0

    lax.fori_loop(0, per, forward, 0, unroll=True)

    ssend[...] = ssc[...].astype(BF16)
    scopies = [
        remote(ssend.at[zpeer(d)], srecv.at[z], s_s.at[d - 1], s_r.at[d - 1], (t, zpeer(d)))
        for d in range(1, n_c)
    ]
    for copy in scopies:
        copy.start()
    srecv[z] = ssend[z]
    for copy in infos:
        copy.wait_recv()
    for copy in scopies:
        copy.wait_recv()

    owners = n_c // n_sets
    step = 16

    def pixels(j, _):
        r = pl.multiple_of(j * step, step)
        sums = []
        for s in range(n_sets):
            total = srecv[s * owners, pl.ds(r, step), :].astype(F32)
            for o in range(1, owners):
                total = total + srecv[s * owners + o, pl.ds(r, step), :].astype(F32)
            sums.append(total)
        goal = target_ref[pl.ds(r, step), :].astype(F32)
        pixel = weight_ref[pl.ds(r, step), :]
        for b in range(n_b):
            cut = slice(b * BLK, (b + 1) * BLK)
            den = jnp.zeros((step, BLK), F32)
            acc = [jnp.zeros((step, BLK), F32) for _ in range(n_sets)]
            tv = goal[:, cut]
            for c in range(n_c * local_corners):
                zc, i = divmod(c, local_corners)
                which = inforecv[zc, 2 * i : 2 * i + 1, cut]
                amount = inforecv[zc, 2 * i + 1 : 2 * i + 2, cut]
                which = jnp.broadcast_to(which, (step, BLK))
                chosen = sums[n_sets - 1][:, cut]
                for s in range(n_sets - 1):
                    chosen = jnp.where(which == float(s), sums[s][:, cut], chosen)
                printed = 1.0 / (1.0 + jnp.exp(print_steep * (print_level - amount * chosen)))
                differ = printed - tv
                err = jnp.exp(lse_sharp * (differ * differ))
                den = den + err
                part = amount * err * differ * (printed * (1.0 - printed))
                for s in range(n_sets):
                    acc[s] = acc[s] + jnp.where(which == float(s), part, 0.0)
            softsend[pl.ds(r, step), cut] = jnp.log(den) / lse_sharp
            scale = (4.0 * print_steep) * pixel[:, cut] / den
            for s in range(n_sets):
                fsend[s, pl.ds(r, step), cut] = (scale * acc[s]).astype(BF16)
        return 0

    lax.fori_loop(0, share // step, pixels, 0)

    fcopies = [
        remote(fsend.at[(zpeer(d) * per) // n_k], frecv.at[z], f_s.at[d - 1], f_r.at[d - 1],
               (t, zpeer(d)))
        for d in range(1, n_c)
    ]
    for copy in fcopies:
        copy.start()
    softs = [
        remote(softsend, softrecv.at[z], soft_s.at[d - 1], soft_r.at[d - 1], (t, zpeer(d)))
        for d in range(1, n_c)
    ]
    frecv[z] = fsend[s_me]
    softrecv[z] = softsend[...]
    for copy in fcopies:
        copy.wait_recv()
    for copy in softs:
        copy.start()

    def backward(k, _):
        factor = frecv[...].reshape(rows, cols).astype(F32) * kw_ref[s_me, k_me + k]
        both = jnp.concatenate([factor, factor], axis=0)
        cot = (both * fields[k].astype(F32)).astype(BF16)
        back = lax.dot_general(
            ra[k], cot, (((0,), (0,)), ((), ())), preferred_element_type=F32
        ).astype(BF16)
        for b in range(n_b):
            for p in range(2):
                piece = back[p * ext : (p + 1) * ext, b * BLK : (b + 1) * BLK]
                at = pl.ds(pl.multiple_of(k * 2 * BLK + p * BLK, BLK), BLK)
                low = b * 2 * reach
                bkr[low : low + reach, at] = piece[0:reach]
                bkr[low + reach : low + 2 * reach, at] = piece[reach + rows : ext]
                bkm[b * rows : (b + 1) * rows, at] = piece[reach : reach + rows]
        return 0

    lax.fori_loop(0, per, backward, 0, unroll=True)

    def column_sum(ref, count):
        g = jnp.dot(ref[...], cb[...], preferred_element_type=F32)
        strips = []
        for j in range(n_b + 1):
            value = None
            if j < n_b:
                value = g[j * count : (j + 1) * count, 0:BLK]
            if j > 0:
                other = g[(j - 1) * count : j * count, BLK : 2 * BLK]
                value = other if value is None else value + other
            strips.append(value)
        wide = jnp.concatenate(strips, axis=1)
        return pltpu.roll(wide, cols + reach, 1)[:, 0:cols]

    rim = column_sum(bkr, 2 * reach)
    rimsend[...] = rim.astype(BF16).reshape(rimsend.shape)
    rim_up = remote(rimsend.at[0], rimrecv.at[0], rim_s.at[0], rim_r.at[0], (tpeer(n_t - 1), z))
    rim_down = remote(rimsend.at[1], rimrecv.at[1], rim_s.at[1], rim_r.at[1], (tpeer(1), z))

    @pl.when(t > 0)
    def _():
        rim_up.start()

    @pl.when(t < n_t - 1)
    def _():
        rim_down.start()

    middle = column_sum(bkm, rows)

    @pl.when(t < n_t - 1)
    def _():
        rim_up.wait_recv()

    @pl.when(t > 0)
    def _():
        rim_down.wait_recv()

    rims = jnp.concatenate([rimrecv[1], rimrecv[0]], axis=0).astype(F32)
    if rows > 2 * reach:
        gap = jnp.zeros((rows - 2 * reach, cols), F32)
        rims = jnp.concatenate([rims[0:reach], gap, rims[reach:]], axis=0)
    gown[...] = (middle + rims).reshape(gown.shape)
    gsend[...] = gown[...].astype(BF16)
    gcopies = [
        remote(gsend.at[zpeer(d)], grecv.at[d - 1], g_s.at[d - 1], g_r.at[d - 1], (t, zpeer(d)))
        for d in range(1, n_c)
    ]
    for copy in gcopies:
        copy.start()
    for copy in softs:
        copy.wait_recv()
    soft_ref[...] = softrecv[...].reshape(rows, cols)
    grad = gown[z]
    for d in range(1, n_c):
        gcopies[d - 1].wait_recv()
        grad = grad + grecv[d - 1].astype(F32)

    square = jnp.sum((grad * grad).reshape(share // 8, 8, cols), axis=0)
    part = square[:, 0:BLK]
    for b in range(1, n_b):
        part = part + square[:, b * BLK : (b + 1) * BLK]
    sqsend[...] = jnp.sum(part, axis=0, keepdims=True)

    def square_copy(d):
        return remote(sqsend, sqrecv.at[d - 1], sq_s.at[d - 1], sq_r.at[d - 1], anyone(d))

    def square_start(d, _):
        square_copy(d).start()
        return 0

    def square_wait(d, _):
        square_copy(d).wait_recv()
        return 0

    lax.fori_loop(1, everyone, square_start, 0, unroll=4)
    lax.fori_loop(1, everyone, square_wait, 0, unroll=4)
    part = sqsend[...] + jnp.sum(sqrecv[...], axis=0)
    total = jnp.sum(part, axis=1, keepdims=True)
    rate = step_rate / jnp.sqrt(total / (rows * n_t * cols) + small_eps)
    own = mask_ref[pl.ds(row0, share), :]
    new_ref[...] = jnp.clip(own - rate * grad, 0.0, 1.0)

    @pl.when(t < n_t - 1)
    def _():
        down.wait_send()
        rim_down.wait_send()

    @pl.when(t > 0)
    def _():
        up.wait_send()
        rim_up.wait_send()

    for copy in infos + scopies + fcopies + softs + gcopies:
        copy.wait_send()

    def square_sent(d, _):
        square_copy(d).wait_send()
        return 0

    lax.fori_loop(1, everyone, square_sent, 0, unroll=4)


def solution(mesh):
    n_t, n_c = mesh.shape["tile"], mesh.shape["corner"]

    def local(mask, target, pixel_weight, row_taps, col_taps, kernel_weights, corner_set, dose):
        rows, cols = mask.shape
        n_sets, n_k, _, taps = row_taps.shape
        reach = (taps - 1) // 2
        ext, win, n_b = rows + 2 * reach, BLK + 2 * reach, cols // BLK
        share = rows // n_c
        per = n_sets * n_k // n_c
        info_rows = 8 * ((2 * corner_set.shape[0] + 7) // 8)
        vmem = pl.BlockSpec(memory_space=pltpu.VMEM)
        hbm = pl.BlockSpec(memory_space=pl.ANY)
        S = pltpu.SMEM
        V = pltpu.VMEM
        dma = pltpu.SemaphoreType.DMA
        zc = dma((n_c - 1,))
        scratch = [
            V((rows, cols), F32),
            V((share, cols), jnp.int32),
            V((share, cols), F32),
            V((n_k, 2, taps), F32),
            V((n_k, 2, taps), F32),
            S((n_sets, n_k), F32),
            S(corner_set.shape, jnp.int32),
            S(dose.shape, F32),
            dma((8,)),
            V((ext, cols + 2 * reach), BF16),
            V((n_b * ext, win), BF16),
            V((8, max(ext, win)), F32),
            V((per, 2 * rows, 2 * ext), BF16),
            V((per * 2 * BLK, win), BF16),
            V((per, win, 2 * BLK), BF16),
            V((per, 2 * ext, cols), BF16),
            V((per, 2 * rows, cols), BF16),
            V((n_c, share, cols), F32),
            V((n_c, share, cols), BF16),
            V((n_c, share, cols), BF16),
            V((info_rows, cols), F32),
            V((n_c, info_rows, cols), F32),
            V((n_sets, share, cols), BF16),
            V((n_c, share, cols), BF16),
            V((share, cols), F32),
            V((n_c, share, cols), F32),
            V((n_b * 2 * reach, per * 2 * BLK), BF16),
            V((n_b * rows, per * 2 * BLK), BF16),
            V((2, reach, cols), BF16),
            V((2, reach, cols), BF16),
            V((n_c, share, cols), F32),
            V((n_c, share, cols), BF16),
            V((n_c - 1, share, cols), BF16),
            V((1, BLK), F32),
            V((n_t * n_c - 1, 1, BLK), F32),
            dma((2,)), dma((2,)),
            zc, zc, zc, zc, zc, zc, zc, zc,
            dma((2,)), dma((2,)),
            zc, zc,
            dma((n_t * n_c - 1,)), dma((n_t * n_c - 1,)),
        ]
        return pl.pallas_call(
            functools.partial(kernel, n_t, n_c),
            out_shape=(
                jax.ShapeDtypeStruct((rows, cols), F32),
                jax.ShapeDtypeStruct((share, cols), F32),
            ),
            in_specs=[hbm] * 8,
            out_specs=(vmem, vmem),
            scratch_shapes=scratch,
            compiler_params=pltpu.CompilerParams(
                collective_id=0, has_side_effects=True, vmem_limit_bytes=60 * 1024 * 1024
            ),
        )(mask, target, pixel_weight, row_taps, col_taps, kernel_weights, corner_set, dose)

    placed = (
        P("tile", None),
        P("tile", None),
        P("tile", None),
        P(),
        P(),
        P(),
        P("corner"),
        P("corner"),
    )
    return jax.shard_map(
        local,
        mesh=mesh,
        in_specs=placed,
        out_specs=(P("tile", None), P(("tile", "corner"), None)),
        check_vma=False,
    )
```
